256 devices in a mesh: wide: 128 (over z, y, x), narrow: 2 (over core).
Axes of the slice: x: 4, y: 4, z: 8, core: 2. Of those that a mesh axis runs over, the one named last changes fastest.
Arguments:
- vectors: bfloat16 [524288, 512], P(('wide', 'narrow')), may hold values from -6 to 6
- leaf_factors: bfloat16 [6, 8192, 64, 128], P(None, ('wide', 'narrow')), may hold values from -0.5 to 0.5
- root_factors: bfloat16 [6, 8192, 64, 128], P(None, ('wide', 'narrow')), may hold values from -0.5 to 0.5
Outputs:
- applied: bfloat16 [524288, 512], P(('wide', 'narrow'))
The draws below stay inside these ranges and needn't reach their ends.
All inputs are finite; a program needn't handle non-finite values.
Results may differ from the reference program's by a relative error of at most 0.024.
Values may be sent and summed in bfloat16 or wider, within the bound.
A program may use at most 64 MiB of HBM per device.

```python
import jax
import jax.numpy as jnp

BLK = 64
BLK_DEV = 32
LOCAL = 5
RHS = 512
LEVELS = 6
ROWS_DEV = 2048
NBLK = 8192
ORDER = 524288
N_WIDE = 128
N_NARROW = 2


def level_of(stream_key, dims, pieces, low, high):
    factor_of, own = 1.0, jax.random.fold_in(stream_key, 6)
    for position, shards_of in pieces:
        heights = jnp.exp(jax.random.uniform(jax.random.fold_in(own, position), (shards_of,), jnp.float32, low / len(pieces), high / len(pieces)))
        factor_of = factor_of * jnp.repeat(heights, dims[position] // shards_of).reshape([-1 if axis == position else 1 for axis in range(len(dims))])
    return factor_of


def centred(stream_key, dims, width, limit, pieces=(), dtype=jnp.bfloat16):
    result = width * jax.random.normal(stream_key, dims, jnp.float32)
    if pieces:
        result = result * level_of(stream_key, dims, pieces, -0.22, 0.18)
    return jnp.clip(result, -limit, limit).astype(dtype)


def setup_inputs(seed: int = 0) -> dict:
    seeds = jax.random.split(jax.random.key(seed), 4)
    vectors = centred(seeds[0], (ORDER, RHS), 1.0, 6.0, ((0, 256),))
    leaf_factors = centred(seeds[1], (LEVELS, NBLK, BLK, 2 * BLK), (2 * BLK) ** -0.5, 0.5, ((1, 256),))
    root_factors = centred(seeds[2], (LEVELS, NBLK, BLK, 2 * BLK), (2 * BLK) ** -0.5, 0.5, ((1, 256),))
    return {"vectors": vectors, "leaf_factors": leaf_factors, "root_factors": root_factors}


def partner_blocks(blocks, stride):
    block_count, block_rows, columns = blocks.shape
    grouped = blocks.reshape(block_count // (2 * stride), 2, stride, block_rows, columns)
    return grouped[:, ::-1].reshape(blocks.shape)


def apply_level(factor, blocks, paired):
    block_rows = blocks.shape[1]
    direct = jnp.einsum("nij,njr->nir", factor[:, :, :block_rows].astype(jnp.float32), blocks.astype(jnp.float32))
    crossed = jnp.einsum("nij,njr->nir", factor[:, :, block_rows:].astype(jnp.float32), paired.astype(jnp.float32))
    return (direct + crossed).astype(jnp.bfloat16)


def reference(vectors, leaf_factors, root_factors):
    blocks = vectors.reshape(NBLK, BLK, RHS)
    for depth in range(LOCAL):
        blocks = apply_level(leaf_factors[depth], blocks, partner_blocks(blocks, 2 ** depth))
    blocks = apply_level(leaf_factors[LOCAL], blocks, partner_blocks(blocks, BLK_DEV))
    moved = blocks.reshape(N_WIDE, N_NARROW, N_WIDE, ROWS_DEV // N_WIDE, RHS)
    moved = jnp.transpose(moved, (2, 1, 0, 3, 4)).reshape(NBLK, BLK, RHS)
    blocks = apply_level(root_factors[0], moved, partner_blocks(moved, BLK_DEV))
    for depth in range(LOCAL):
        blocks = apply_level(root_factors[depth + 1], blocks, partner_blocks(blocks, 2 ** depth))
    return blocks.reshape(ORDER, RHS)
```

```python
import jax
import jax.numpy as jnp
from jax import lax
from jax.experimental import pallas as pl
from jax.experimental.pallas import tpu as pltpu
from jax.sharding import PartitionSpec as P

MESH = pl.DeviceIdType.MESH
NZ, NY, NX = 8, 4, 4
PLANE = NY * NX
BLOCKS, BLK, ROWS, COLS, CHUNKS = 32, 64, 16, 128, 4
GROUP = BLOCKS // NZ
LEVELS = 6
PLANE_FIRST = (False, False, True, True)
Z_ORDER = (4, 5, 1, 2, 6, 3, 7)


def swap_halves(factor):
    return jnp.concatenate([factor[:, BLK:], factor[:, :BLK]], axis=1)


def product(factor, blocks):
    return jnp.dot(factor, blocks, preferred_element_type=jnp.float32).astype(jnp.bfloat16)


def pair_level(factors, source, target, low, stride):
    high = low + stride
    out = product(
        jnp.concatenate([factors[low], factors[high]], axis=0),
        jnp.concatenate([source[low], source[high]], axis=0),
    )
    target[low] = out[:BLK]
    target[high] = out[BLK:]


def first_of_pair(index, stride):
    return (index // stride) * (2 * stride) + index % stride


def kernel(
    vectors, leaf_hbm, root_hbm, out_hbm,
    leaf, root, ping, pong, other, leafed, half, moved, moved_other, ping2, pong2, result,
    sem_vec, sem_leaf, sem_root, sem_out, sem_own,
    pair_send, pair_recv, z_send, z_recv, plane_send, plane_recv, pair2_send, pair2_recv,
):
    wide = lax.axis_index("wide")
    core = lax.axis_index("narrow")
    z, y, x = wide // PLANE, (wide // NX) % NY, wide % NX
    plane = wide % PLANE
    partner = (wide, 1 - core)

    def at_z(offset):
        return (z + offset) % NZ

    def z_device(offset):
        return (at_z(offset) * PLANE + plane, core)

    def plane_at(offset):
        return ((y + offset // NX) % NY) * NX + (x + offset % NX) % NX

    def plane_device(offset):
        return (z * PLANE + plane_at(offset), core)

    loads = []
    def load_vec(c):
        return pltpu.make_async_copy(
            vectors.at[:, :, pl.ds(c * COLS, COLS)], ping.at[c], sem_vec.at[c])

    def load_leaf(l):
        return pltpu.make_async_copy(leaf_hbm.at[l], leaf.at[l], sem_leaf.at[l])

    def load_root(l):
        return pltpu.make_async_copy(root_hbm.at[l], root.at[l], sem_root.at[l])

    load_vec(0).start()
    for l in range(LEVELS):
        load_leaf(l).start()
    for c in range(1, CHUNKS):
        load_vec(c).start()
    for l in range(LEVELS):
        load_root(l).start()

    barrier = pltpu.get_barrier_semaphore()
    pl.semaphore_signal(barrier, inc=1, device_id=partner, device_id_type=MESH)
    for d in range(1, NZ):
        pl.semaphore_signal(barrier, inc=1, device_id=z_device(d), device_id_type=MESH)

    @pl.loop(1, PLANE)
    def _(j):
        pl.semaphore_signal(barrier, inc=1, device_id=plane_device(j), device_id_type=MESH)

    def prepare(factors, stride):
        for q in range(BLOCKS // 2):
            high = first_of_pair(q, stride) + stride
            factors[high] = swap_halves(factors[high])

    def pair_copy(c, i, k):
        return pltpu.make_async_remote_copy(
            pong.at[c, :, pl.ds(i * GROUP, GROUP)], other.at[c, :, pl.ds(i * GROUP, GROUP)],
            pair_send.at[c, k], pair_recv.at[c, k], device_id=partner, device_id_type=MESH)

    def z_copy(c, d):
        source, target = (half, moved) if PLANE_FIRST[c] else (leafed, half)
        return pltpu.make_async_remote_copy(
            source.at[c, at_z(d)], target.at[c, z], z_send.at[c, d - 1], z_recv.at[c, d - 1],
            device_id=z_device(d), device_id_type=MESH)

    def z_own(c):
        source, target = (half, moved) if PLANE_FIRST[c] else (leafed, half)
        return pltpu.make_async_copy(source.at[c, z], target.at[c, z], sem_own.at[c, 0])

    def plane_copy(c, j):
        source, target = (leafed, half) if PLANE_FIRST[c] else (half, moved)
        return pltpu.make_async_remote_copy(
            source.at[c, :, plane_at(j)], target.at[c, :, plane], plane_send.at[c], plane_recv.at[c],
            device_id=plane_device(j), device_id_type=MESH)

    def plane_all(c):
        source, target = (leafed, half) if PLANE_FIRST[c] else (half, moved)
        return pltpu.make_async_remote_copy(
            source.at[c, :, pl.ds(0, PLANE - 1)], target.at[c, :, pl.ds(0, PLANE - 1)],
            plane_send.at[c], plane_recv.at[c], device_id=partner, device_id_type=MESH)

    def plane_own(c):
        source, target = (leafed, half) if PLANE_FIRST[c] else (half, moved)
        return pltpu.make_async_copy(source.at[c, :, plane], target.at[c, :, plane], sem_own.at[c, 1])

    def plane_start(c):
        @pl.loop(1, PLANE)
        def _(j):
            plane_copy(c, j).start()
        plane_own(c).start()

    def plane_wait(c):
        plane_own(c).wait()
        plane_all(c).wait_recv()

    def z_start(c):
        for d in Z_ORDER:
            z_copy(c, d).start()
        z_own(c).start()

    def pair2_copy(c, zs, k):
        return pltpu.make_async_remote_copy(
            moved.at[c, zs], moved_other.at[c, zs], pair2_send.at[c, k], pair2_recv.at[c, k],
            device_id=partner, device_id_type=MESH)

    def out_copy(c):
        return pltpu.make_async_copy(result.at[c], out_hbm.at[:, :, pl.ds(c * COLS, COLS)], sem_out.at[c])

    def whole_level(factors, source, target, stride):
        for q in range(BLOCKS // 2):
            pair_level(factors, source, target, first_of_pair(q, stride), stride)

    def leaf_levels(c):
        load_vec(c).wait()
        source, target = ping.at[c], pong.at[c]
        flat = pong.at[c]
        for l in range(4):
            if c == 0:
                load_leaf(l).wait()
                prepare(leaf.at[l], 1 << l)
            a = ping.at[c] if l % 2 == 0 else pong.at[c].reshape(BLOCKS, BLK, COLS)
            b = pong.at[c].reshape(BLOCKS, BLK, COLS) if l % 2 == 0 else ping.at[c]
            whole_level(leaf.at[l], a, b, 1 << l)
        if c == 0:
            load_leaf(4).wait()
            prepare(leaf.at[4], 16)
            load_leaf(5).wait()
            pl.semaphore_wait(barrier, 1 + (NZ - 1) + (PLANE - 1))
        for k in range(4):
            i = (z + k) % 4
            for q in range(GROUP):
                pair_level(leaf.at[4], ping.at[c], pong.at[c].reshape(BLOCKS, BLK, COLS), i * GROUP + q, 16)
            pair_copy(c, i, k).start()

    def leaf_last(c):
        mine = pong.at[c].reshape(BLOCKS, BLK, COLS)
        theirs = other.at[c].reshape(BLOCKS, BLK, COLS)
        target = leafed.at[c].reshape(BLOCKS, BLK, COLS)
        for k in range(4):
            pair_copy(c, (z + k) % 4, k).wait_recv()
            for d in (k + 4, k):
                for q in range(GROUP):
                    b = at_z(d) * GROUP + q
                    target[b] = product(leaf[5, b], jnp.concatenate([mine[b], theirs[b]], axis=0))
                if d != 0 and not PLANE_FIRST[c]:
                    z_copy(c, d).start()
        if PLANE_FIRST[c]:
            plane_start(c)
        else:
            z_own(c).start()

    def root_group(c, zs):
        mine = moved.at[c].reshape(BLOCKS, BLK, COLS)
        theirs = moved_other.at[c].reshape(BLOCKS, BLK, COLS)
        for q in range(GROUP):
            b = zs * GROUP + q
            ping2[b] = product(root[0, b], jnp.concatenate([mine[b], theirs[b]], axis=0))
        for q in (0, 2):
            pair_level(root.at[1], ping2, pong2, zs * GROUP + q, 1)
        for q in (0, 1):
            pair_level(root.at[2], pong2, ping2, zs * GROUP + q, 2)

    def root_rest(c):
        whole_level(root.at[3], ping2, pong2, 4)
        whole_level(root.at[4], pong2, ping2, 8)
        whole_level(root.at[5], ping2, result.at[c], 16)
        out_copy(c).start()

    def root_plane_last(c):
        plane_wait(c)
        for k in range(NZ):
            pair2_copy(c, k, k).start()
        for k in range(NZ):
            pair2_copy(c, k, k).wait_recv()
            root_group(c, k)
        root_rest(c)

    def root_z_last(c):
        order = (0,) + Z_ORDER
        for n, d in enumerate(order):
            if d == 0:
                z_own(c).wait()
            else:
                z_copy(c, d).wait_recv()
            pair2_copy(c, (z - d) % NZ, d).start()
            if n:
                e = order[n - 1]
                pair2_copy(c, (z - e) % NZ, e).wait_recv()
                root_group(c, (z - e) % NZ)
        e = order[-1]
        pair2_copy(c, (z - e) % NZ, e).wait_recv()
        root_group(c, (z - e) % NZ)
        root_rest(c)

    def z_wait(c):
        z_own(c).wait()
        for d in Z_ORDER:
            z_copy(c, d).wait_recv()

    for c in range(CHUNKS):
        leaf_levels(c)
        leaf_last(c)
    for l in range(LEVELS):
        load_root(l).wait()
        if l:
            prepare(root.at[l], 1 << (l - 1))

    z_wait(0)
    plane_start(0)
    plane_wait(2)
    z_start(2)
    z_wait(1)
    plane_start(1)
    plane_wait(3)
    z_start(3)
    root_plane_last(0)
    root_plane_last(1)
    root_z_last(2)
    root_z_last(3)

    for c in range(CHUNKS):
        for k in range(4):
            pair_copy(c, (z + k) % 4, k).wait_send()
        for d in Z_ORDER:
            z_copy(c, d).wait_send()
        plane_all(c).wait_send()
        for k in range(NZ):
            pair2_copy(c, k, k).wait_send()
        out_copy(c).wait()


def per_device(vectors, leaf_factors, root_factors):
    vectors = vectors.reshape(BLOCKS, BLK, CHUNKS * COLS)
    dma = pltpu.SemaphoreType.DMA
    wide_shape = (CHUNKS, BLOCKS, BLK, COLS)
    spread = (CHUNKS, NZ, PLANE, ROWS, COLS)
    halves = (CHUNKS, 2, BLOCKS // 2, BLK, COLS)
    bf = jnp.bfloat16
    vmem = pltpu.VMEM
    out = pl.pallas_call(
        kernel,
        out_shape=jax.ShapeDtypeStruct(vectors.shape, bf),
        in_specs=[pl.BlockSpec(memory_space=pl.ANY)] * 3,
        out_specs=pl.BlockSpec(memory_space=pl.ANY),
        scratch_shapes=[
            vmem((LEVELS, BLOCKS, BLK, 2 * BLK), bf),
            vmem((LEVELS, BLOCKS, BLK, 2 * BLK), bf),
            vmem(wide_shape, bf), vmem(halves, bf), vmem(halves, bf),
            vmem(spread, bf), vmem(spread, bf), vmem(spread, bf), vmem(spread, bf),
            vmem(wide_shape[1:], bf), vmem(wide_shape[1:], bf), vmem(wide_shape, bf),
            dma((CHUNKS,)), dma((LEVELS,)), dma((LEVELS,)), dma((CHUNKS,)), dma((CHUNKS, 2)),
            dma((CHUNKS, 4)), dma((CHUNKS, 4)), dma((CHUNKS, NZ - 1)), dma((CHUNKS, NZ - 1)),
            dma((CHUNKS,)), dma((CHUNKS,)), dma((CHUNKS, NZ)), dma((CHUNKS, NZ)),
        ],
        compiler_params=pltpu.CompilerParams(
            collective_id=0, has_side_effects=True, vmem_limit_bytes=48 * 1024 * 1024),
        name="butterfly",
    )(vectors, leaf_factors, root_factors)
    return out.reshape(BLOCKS * BLK, CHUNKS * COLS)


def solution(mesh):
    in_specs = (
        P(("wide", "narrow"), None),
        P(None, ("wide", "narrow"), None, None),
        P(None, ("wide", "narrow"), None, None),
    )
    out_specs = P(("wide", "narrow"), None)
    return jax.shard_map(
        per_device, mesh=mesh, in_specs=in_specs, out_specs=out_specs, check_vma=False
    )
```

```python
import jax
import jax.numpy as jnp
from jax import lax
from jax.experimental import pallas as pl
from jax.experimental.pallas import tpu as pltpu
from jax.sharding import PartitionSpec as P

MESH = pl.DeviceIdType.MESH
NZ, NY, NX = 8, 4, 4
PLANE = NY * NX
BLOCKS, BLK, ROWS, COLS, CHUNKS = 32, 64, 16, 128, 4
GROUP = BLOCKS // NZ
LEVELS = 6
PLANE_FIRST = (False, True, True, True)
Z_ORDER = (4, 5, 3, 1, 7, 2, 6)
FAR, NEAR = (4, 5, 3), (1, 7, 2, 6)
BATCHES = ((0,) + FAR, NEAR)
EARLY = 2
RUN = ("L0", "L1", "L2", "L3", "P", "R0", "R1", "R2", "R3")
own_copy = pltpu.make_async_copy


def swap_halves(factor):
    return jnp.concatenate([factor[:, BLK:], factor[:, :BLK]], axis=1)


def product(factor, blocks):
    return jnp.dot(factor, blocks, preferred_element_type=jnp.float32).astype(jnp.bfloat16)


def pair_level(factors, source, target, low, stride):
    high = low + stride
    out = product(
        jnp.concatenate([factors[low], factors[high]], axis=0),
        jnp.concatenate([source[low], source[high]], axis=0),
    )
    target[low] = out[:BLK]
    target[high] = out[BLK:]


def first_of_pair(index, stride):
    return (index // stride) * (2 * stride) + index % stride


def kernel(
    vectors, leaf_hbm, root_hbm, out,
    leaf, root, ping, pong, other, leafed, half, moved, moved_other, ping2, pong2,
    sem_vec, sem_leaf, sem_root, sem_own,
    pair_send, pair_recv, z_send, z_recv, plane_send, plane_recv, pair2_send, pair2_recv,
):
    wide = lax.axis_index("wide")
    core = lax.axis_index("narrow")
    z, y, x = wide // PLANE, (wide // NX) % NY, wide % NX
    plane = wide % PLANE
    partner = (wide, 1 - core)

    def at_z(offset):
        return (z + offset) % NZ

    def z_device(offset):
        return (at_z(offset) * PLANE + plane, core)

    def plane_at(offset):
        return ((y + offset // NX) % NY) * NX + (x + offset % NX) % NX

    def plane_device(offset):
        return (z * PLANE + plane_at(offset), core)

    def load_vec(c):
        return pltpu.make_async_copy(
            vectors.at[:, :, pl.ds(c * COLS, COLS)], ping.at[c], sem_vec.at[c])

    def load_leaf(l):
        return pltpu.make_async_copy(leaf_hbm.at[l], leaf.at[l], sem_leaf.at[l])

    def load_root(l):
        return pltpu.make_async_copy(root_hbm.at[l], root.at[l], sem_root.at[l])

    load_vec(0).start()
    for l in range(EARLY):
        load_leaf(l).start()

    barrier = pltpu.get_barrier_semaphore()
    pl.semaphore_signal(barrier, inc=1, device_id=partner, device_id_type=MESH)
    for d in range(1, NZ):
        pl.semaphore_signal(barrier, inc=1, device_id=z_device(d), device_id_type=MESH)

    @pl.loop(1, PLANE)
    def _(j):
        pl.semaphore_signal(barrier, inc=1, device_id=plane_device(j), device_id_type=MESH)

    def prepare(factors, stride):
        for q in range(BLOCKS // 2):
            high = first_of_pair(q, stride) + stride
            factors[high] = swap_halves(factors[high])

    def pair_copy(c, i, k):
        return pltpu.make_async_remote_copy(
            pong.at[c, :, pl.ds(i * GROUP, GROUP)], other.at[c, :, pl.ds(i * GROUP, GROUP)],
            pair_send.at[c, k], pair_recv.at[c, k], device_id=partner, device_id_type=MESH)

    def z_copy(c, d):
        source, target = (half, moved) if PLANE_FIRST[c] else (leafed, half)
        return pltpu.make_async_remote_copy(
            source.at[c, at_z(d)], target.at[c, z], z_send.at[c, d - 1], z_recv.at[c, d - 1],
            device_id=z_device(d), device_id_type=MESH)

    def z_own(c):
        source, target = (half, moved) if PLANE_FIRST[c] else (leafed, half)
        return own_copy(source.at[c, z], target.at[c, z], sem_own.at[c, 0])

    def plane_copy(c, j):
        source, target = (leafed, half) if PLANE_FIRST[c] else (half, moved)
        return pltpu.make_async_remote_copy(
            source.at[c, :, plane_at(j)], target.at[c, :, plane], plane_send.at[c], plane_recv.at[c],
            device_id=plane_device(j), device_id_type=MESH)

    def plane_all(c):
        source, target = (leafed, half) if PLANE_FIRST[c] else (half, moved)
        return pltpu.make_async_remote_copy(
            source.at[c, :, pl.ds(0, PLANE - 1)], target.at[c, :, pl.ds(0, PLANE - 1)],
            plane_send.at[c], plane_recv.at[c], device_id=partner, device_id_type=MESH)

    def plane_own(c):
        source, target = (leafed, half) if PLANE_FIRST[c] else (half, moved)
        return own_copy(source.at[c, :, plane], target.at[c, :, plane], sem_own.at[c, 1])

    def plane_start(c):
        @pl.loop(1, PLANE)
        def _(j):
            plane_copy(c, j).start()
        plane_own(c).start()

    def plane_wait(c):
        plane_own(c).wait()
        plane_all(c).wait_recv()

    def z_start(c, offsets):
        for d in offsets:
            z_copy(c, d).start()

    def pair2_copy(c, zs, k):
        return pltpu.make_async_remote_copy(
            moved.at[c, zs], moved_other.at[c, zs], pair2_send.at[c, k], pair2_recv.at[c, k],
            device_id=partner, device_id_type=MESH)

    def whole_level(factors, source, target, stride):
        for q in range(BLOCKS // 2):
            pair_level(factors, source, target, first_of_pair(q, stride), stride)

    def leaf_levels(c):
        load_vec(c).wait()
        for l in range(4):
            if c == 0:
                load_leaf(l).wait()
                if l == 0:
                    for m in range(EARLY, LEVELS):
                        load_leaf(m).start()
                prepare(leaf.at[l], 1 << l)
            a = ping.at[c] if l % 2 == 0 else pong.at[c].reshape(BLOCKS, BLK, COLS)
            b = pong.at[c].reshape(BLOCKS, BLK, COLS) if l % 2 == 0 else ping.at[c]
            whole_level(leaf.at[l], a, b, 1 << l)
        if c == 0:
            load_leaf(4).wait()
            prepare(leaf.at[4], 16)
            load_leaf(5).wait()
            for m in range(1, CHUNKS):
                load_vec(m).start()
            pl.semaphore_wait(barrier, 1 + (NZ - 1) + (PLANE - 1))
        for k in range(4):
            i = (z + k) % 4
            for q in range(GROUP):
                pair_level(leaf.at[4], ping.at[c], pong.at[c].reshape(BLOCKS, BLK, COLS), i * GROUP + q, 16)
            pair_copy(c, i, k).start()

    def leaf_last(c):
        mine = pong.at[c].reshape(BLOCKS, BLK, COLS)
        theirs = other.at[c].reshape(BLOCKS, BLK, COLS)
        target = leafed.at[c].reshape(BLOCKS, BLK, COLS)
        for k, offsets in enumerate(((4,), (5, 1), (6, 2), (7, 3, 0))):
            pair_copy(c, (z + k) % 4, k).wait_recv()
            for d in offsets:
                for q in range(GROUP):
                    b = at_z(d) * GROUP + q
                    target[b] = product(leaf[5, b], jnp.concatenate([mine[b], theirs[b]], axis=0))
                if d != 0 and not PLANE_FIRST[c]:
                    z_copy(c, d).start()
        if not PLANE_FIRST[c]:
            z_own(c).start()

    def root_groups(c, groups):
        mine = moved.at[c].reshape(BLOCKS, BLK, COLS)
        theirs = moved_other.at[c].reshape(BLOCKS, BLK, COLS)
        for zs in groups:
            for q in range(GROUP):
                b = zs * GROUP + q
                ping2[b] = product(root[0, b], jnp.concatenate([mine[b], theirs[b]], axis=0))
        for zs in groups:
            for q in (0, 2):
                pair_level(root.at[1], ping2, pong2, zs * GROUP + q, 1)
        for zs in groups:
            for q in (0, 1):
                pair_level(root.at[2], pong2, ping2, zs * GROUP + q, 2)

    def root_rest(c):
        whole_level(root.at[3], ping2, pong2, 4)
        whole_level(root.at[4], pong2, ping2, 8)
        whole_level(root.at[5], ping2, out.at[:, :, pl.ds(c * COLS, COLS)], 16)

    def root_exchange(c):
        for k in range(NZ):
            pair2_copy(c, k, k).start()

    def root_plane_last(c):
        for batch in (range(4), range(4, 8)):
            for k in batch:
                pair2_copy(c, k, k).wait_recv()
            root_groups(c, batch)
        root_rest(c)

    def root_z_last(c):
        for batch in BATCHES:
            for d in batch:
                if d == 0:
                    z_own(c).wait()
                else:
                    z_copy(c, d).wait_recv()
                pair2_copy(c, (z - d) % NZ, d).start()
            for d in batch:
                pair2_copy(c, (z - d) % NZ, d).wait_recv()
            root_groups(c, [(z - d) % NZ for d in batch])
        root_rest(c)

    def z_wait(c):
        z_own(c).wait()
        for d in Z_ORDER:
            z_copy(c, d).wait_recv()

    def leaf_section(c):
        if f"L{c}" in RUN:
            leaf_levels(c)
            leaf_last(c)
        else:
            load_vec(c).wait()
            if c == 0:
                for l in range(LEVELS):
                    load_leaf(l).wait()

    def root_section(c):
        if f"R{c}" in RUN:
            (root_z_last if PLANE_FIRST[c] else root_plane_last)(c)

    leaf_section(0)
    for l in range(LEVELS):
        load_root(l).start()
    leaf_section(1)
    plane_start(1)
    leaf_section(2)
    leaf_section(3)
    for l in range(LEVELS):
        load_root(l).wait()
        if l and "P" in RUN:
            prepare(root.at[l], 1 << (l - 1))
    plane_wait(1)
    z_start(1, Z_ORDER)
    z_own(1).start()
    plane_start(2)
    z_wait(0)
    plane_start(0)
    plane_wait(2)
    z_start(2, Z_ORDER)
    z_own(2).start()
    plane_wait(0)
    plane_start(3)
    root_exchange(0)
    root_section(0)
    root_section(1)
    plane_wait(3)
    z_start(3, FAR)
    z_own(3).start()
    root_section(2)
    z_start(3, NEAR)
    root_section(3)

    for c in range(CHUNKS):
        for k in range(4):
            pair_copy(c, (z + k) % 4, k).wait_send()
        for d in Z_ORDER:
            z_copy(c, d).wait_send()
        plane_all(c).wait_send()
        for k in range(NZ):
            pair2_copy(c, k, k).wait_send()


def per_device(vectors, leaf_factors, root_factors):
    vectors = vectors.reshape(BLOCKS, BLK, CHUNKS * COLS)
    dma = pltpu.SemaphoreType.DMA
    wide_shape = (CHUNKS, BLOCKS, BLK, COLS)
    spread = (CHUNKS, NZ, PLANE, ROWS, COLS)
    halves = (CHUNKS, 2, BLOCKS // 2, BLK, COLS)
    bf = jnp.bfloat16
    vmem = pltpu.VMEM
    out = pl.pallas_call(
        kernel,
        out_shape=jax.ShapeDtypeStruct(vectors.shape, bf),
        in_specs=[pl.BlockSpec(memory_space=pltpu.HBM)] * 3,
        out_specs=pl.BlockSpec(memory_space=pltpu.VMEM),
        scratch_shapes=[
            vmem((LEVELS, BLOCKS, BLK, 2 * BLK), bf),
            vmem((LEVELS, BLOCKS, BLK, 2 * BLK), bf),
            vmem(wide_shape, bf), vmem(halves, bf), vmem(halves, bf),
            vmem(spread, bf), vmem(spread, bf), vmem(spread, bf), vmem(spread, bf),
            vmem(wide_shape[1:], bf), vmem(wide_shape[1:], bf),
            dma((CHUNKS,)), dma((LEVELS,)), dma((LEVELS,)), dma((CHUNKS, 2)),
            dma((CHUNKS, 4)), dma((CHUNKS, 4)), dma((CHUNKS, NZ - 1)), dma((CHUNKS, NZ - 1)),
            dma((CHUNKS,)), dma((CHUNKS,)), dma((CHUNKS, NZ)), dma((CHUNKS, NZ)),
        ],
        compiler_params=pltpu.CompilerParams(
            collective_id=0, has_side_effects=True, vmem_limit_bytes=48 * 1024 * 1024),
        name="butterfly",
    )(vectors, leaf_factors, root_factors)
    return out.reshape(BLOCKS * BLK, CHUNKS * COLS)


def solution(mesh):
    in_specs = (
        P(("wide", "narrow"), None),
        P(None, ("wide", "narrow"), None, None),
        P(None, ("wide", "narrow"), None, None),
    )
    out_specs = P(("wide", "narrow"), None)
    return jax.shard_map(
        per_device, mesh=mesh, in_specs=in_specs, out_specs=out_specs, check_vma=False
    )
```

```python
import jax
import jax.numpy as jnp
from jax import lax
from jax.experimental import pallas as pl
from jax.experimental.pallas import tpu as pltpu
from jax.sharding import PartitionSpec as P

MESH = pl.DeviceIdType.MESH
NZ, NY, NX = 8, 4, 4
PLANE = NY * NX
BLOCKS, BLK, ROWS, COLS, CHUNKS = 32, 64, 16, 128, 4
GROUP = BLOCKS // NZ
LEVELS = 6
PLANE_FIRST = (False, True, True, True)
Z_ORDER = (4, 5, 3, 1, 7, 2, 6)
FAR, NEAR = (4, 5, 3), (1, 7, 2, 6)
BATCHES = ((0,) + NEAR + FAR,)
EARLY = 2
UNROLL = 16
LOOP = True


def in_hbm(array):
    return pltpu.with_memory_space_constraint(array, pltpu.HBM)


RUN = ("L0", "L1", "L2", "L3", "P", "R0", "R1", "R2", "R3")
own_copy = pltpu.make_async_copy


def plane_first(c):
    return PLANE_FIRST[c] if isinstance(c, int) else True


def swap_halves(factor):
    return jnp.concatenate([factor[:, BLK:], factor[:, :BLK]], axis=1)


def product(factor, blocks):
    return jnp.dot(factor, blocks, preferred_element_type=jnp.float32).astype(jnp.bfloat16)


def pair_level(factors, source, target, low, stride):
    high = low + stride
    out = product(
        jnp.concatenate([factors[low], factors[high]], axis=0),
        jnp.concatenate([source[low], source[high]], axis=0),
    )
    target[low] = out[:BLK]
    target[high] = out[BLK:]


def first_of_pair(index, stride):
    return (index // stride) * (2 * stride) + index % stride


def kernel(
    vectors, leaf_hbm, root_hbm, out,
    leaf, root, ping, pong, other, leafed, half, moved, moved_other, ping2, pong2,
    sem_vec, sem_leaf, sem_root, sem_own,
    pair_send, pair_recv, z_send, z_recv, plane_send, plane_recv, pair2_send, pair2_recv,
):
    wide = lax.axis_index("wide")
    core = lax.axis_index("narrow")
    z, y, x = wide // PLANE, (wide // NX) % NY, wide % NX
    plane = wide % PLANE
    partner = (wide, 1 - core)

    def at_z(offset):
        return (z + offset) % NZ

    def z_device(offset):
        return (at_z(offset) * PLANE + plane, core)

    def plane_at(offset):
        return ((y + offset // NX) % NY) * NX + (x + offset % NX) % NX

    def plane_device(offset):
        return (z * PLANE + plane_at(offset), core)

    def load_vec(c):
        return pltpu.make_async_copy(
            vectors.at[:, :, pl.ds(c * COLS, COLS)], ping.at[c], sem_vec.at[c])

    def load_leaf(l):
        return pltpu.make_async_copy(leaf_hbm.at[l], leaf.at[l], sem_leaf.at[l])

    def load_root(l):
        return pltpu.make_async_copy(root_hbm.at[l], root.at[l], sem_root.at[l])

    load_vec(0).start()
    for l in range(EARLY):
        load_leaf(l).start()

    barrier = pltpu.get_barrier_semaphore()
    pl.semaphore_signal(barrier, inc=1, device_id=partner, device_id_type=MESH)
    for d in range(1, NZ):
        pl.semaphore_signal(barrier, inc=1, device_id=z_device(d), device_id_type=MESH)

    @pl.loop(1, PLANE)
    def _(j):
        pl.semaphore_signal(barrier, inc=1, device_id=plane_device(j), device_id_type=MESH)

    def prepare(factors, stride):
        for q in range(BLOCKS // 2):
            high = first_of_pair(q, stride) + stride
            factors[high] = swap_halves(factors[high])

    def pair_copy(c, i, k):
        return pltpu.make_async_remote_copy(
            pong.at[c, :, pl.ds(i * GROUP, GROUP)], other.at[c, :, pl.ds(i * GROUP, GROUP)],
            pair_send.at[c, k], pair_recv.at[c, k], device_id=partner, device_id_type=MESH)

    def z_copy(c, d):
        source, target = (half, moved) if plane_first(c) else (leafed, half)
        return pltpu.make_async_remote_copy(
            source.at[c, at_z(d)], target.at[c, z], z_send.at[c, d - 1], z_recv.at[c, d - 1],
            device_id=z_device(d), device_id_type=MESH)

    def z_own(c):
        source, target = (half, moved) if plane_first(c) else (leafed, half)
        return own_copy(source.at[c, z], target.at[c, z], sem_own.at[c, 0])

    def plane_copy(c, j):
        source, target = (leafed, half) if plane_first(c) else (half, moved)
        return pltpu.make_async_remote_copy(
            source.at[c, :, plane_at(j)], target.at[c, :, plane], plane_send.at[c], plane_recv.at[c],
            device_id=plane_device(j), device_id_type=MESH)

    def plane_all(c):
        source, target = (leafed, half) if plane_first(c) else (half, moved)
        return pltpu.make_async_remote_copy(
            source.at[c, :, pl.ds(0, PLANE - 1)], target.at[c, :, pl.ds(0, PLANE - 1)],
            plane_send.at[c], plane_recv.at[c], device_id=partner, device_id_type=MESH)

    def plane_own(c):
        source, target = (leafed, half) if plane_first(c) else (half, moved)
        return own_copy(source.at[c, :, plane], target.at[c, :, plane], sem_own.at[c, 1])

    def plane_start(c):
        @pl.loop(1, PLANE)
        def _(j):
            plane_copy(c, j).start()
        plane_own(c).start()

    def plane_wait(c):
        plane_own(c).wait()
        plane_all(c).wait_recv()

    def z_start(c, offsets):
        for d in offsets:
            z_copy(c, d).start()

    def pair2_copy(c, zs, k):
        return pltpu.make_async_remote_copy(
            moved.at[c, zs], moved_other.at[c, zs], pair2_send.at[c, k], pair2_recv.at[c, k],
            device_id=partner, device_id_type=MESH)

    def whole_level(factors, source, target, stride):
        if UNROLL == 16:
            for q in range(BLOCKS // 2):
                pair_level(factors, source, target, first_of_pair(q, stride), stride)
            return

        @pl.loop(0, BLOCKS // 2 // UNROLL)
        def _(i):
            for q in range(UNROLL):
                pair_level(factors, source, target, first_of_pair(i * UNROLL + q, stride), stride)

    def leaf_levels(c):
        load_vec(c).wait()
        for l in range(4):
            if c == 0:
                load_leaf(l).wait()
                if l == 0:
                    for m in range(EARLY, LEVELS):
                        load_leaf(m).start()
                prepare(leaf.at[l], 1 << l)
            a = ping.at[c] if l % 2 == 0 else pong.at[c].reshape(BLOCKS, BLK, COLS)
            b = pong.at[c].reshape(BLOCKS, BLK, COLS) if l % 2 == 0 else ping.at[c]
            whole_level(leaf.at[l], a, b, 1 << l)
        if c == 0:
            load_leaf(4).wait()
            prepare(leaf.at[4], 16)
            load_leaf(5).wait()
            for m in range(1, CHUNKS):
                load_vec(m).start()
            pl.semaphore_wait(barrier, 1 + (NZ - 1) + (PLANE - 1))
        for k in range(4):
            i = (z + k) % 4
            for q in range(GROUP):
                pair_level(leaf.at[4], ping.at[c], pong.at[c].reshape(BLOCKS, BLK, COLS), i * GROUP + q, 16)
            pair_copy(c, i, k).start()

    def leaf_last(c):
        mine = pong.at[c].reshape(BLOCKS, BLK, COLS)
        theirs = other.at[c].reshape(BLOCKS, BLK, COLS)
        target = leafed.at[c].reshape(BLOCKS, BLK, COLS)
        for k, offsets in enumerate(((4,), (5, 1), (6, 2), (7, 3, 0))):
            pair_copy(c, (z + k) % 4, k).wait_recv()
            for d in offsets:
                for q in range(GROUP):
                    b = at_z(d) * GROUP + q
                    target[b] = product(leaf[5, b], jnp.concatenate([mine[b], theirs[b]], axis=0))
                if d != 0 and not PLANE_FIRST[c]:
                    z_copy(c, d).start()
        if not PLANE_FIRST[c]:
            z_own(c).start()

    def root_groups(c, groups):
        mine = moved.at[c].reshape(BLOCKS, BLK, COLS)
        theirs = moved_other.at[c].reshape(BLOCKS, BLK, COLS)
        for zs in groups:
            for q in range(GROUP):
                b = zs * GROUP + q
                ping2[b] = product(root[0, b], jnp.concatenate([mine[b], theirs[b]], axis=0))
        for zs in groups:
            for q in (0, 2):
                pair_level(root.at[1], ping2, pong2, zs * GROUP + q, 1)
        for zs in groups:
            for q in (0, 1):
                pair_level(root.at[2], pong2, ping2, zs * GROUP + q, 2)

    def root_rest(c):
        whole_level(root.at[3], ping2, pong2, 4)
        whole_level(root.at[4], pong2, ping2, 8)
        whole_level(root.at[5], ping2, out.at[:, :, pl.ds(pl.multiple_of(c * COLS, COLS) if not isinstance(c, int) else c * COLS, COLS)], 16)

    def root_exchange(c):
        for k in range(NZ):
            pair2_copy(c, k, k).start()

    def root_plane_last(c):
        for batch in (range(4), range(4, 8)):
            for k in batch:
                pair2_copy(c, k, k).wait_recv()
            root_groups(c, batch)
        root_rest(c)

    def root_z_last(c):
        for d in sum(BATCHES, ()):
            if d == 0:
                z_own(c).wait()
            else:
                z_copy(c, d).wait_recv()
            pair2_copy(c, (z - d) % NZ, d).start()
        for batch in BATCHES:
            for d in batch:
                pair2_copy(c, (z - d) % NZ, d).wait_recv()
            root_groups(c, [(z - d) % NZ for d in batch])
        root_rest(c)

    def z_wait(c):
        z_own(c).wait()
        for d in Z_ORDER:
            z_copy(c, d).wait_recv()

    def leaf_section(c):
        if f"L{c}" in RUN:
            leaf_levels(c)
            leaf_last(c)
        else:
            load_vec(c).wait()
            if c == 0:
                for l in range(LEVELS):
                    load_leaf(l).wait()

    def root_section(c):
        if f"R{c}" in RUN:
            (root_z_last if plane_first(c) else root_plane_last)(c)

    leaf_section(0)
    for l in range(LEVELS):
        load_root(l).start()
    leaf_section(1)
    plane_start(1)
    leaf_section(2)
    leaf_section(3)
    for l in range(LEVELS):
        load_root(l).wait()
        if l and "P" in RUN:
            prepare(root.at[l], 1 << (l - 1))
    plane_wait(1)
    z_start(1, Z_ORDER)
    z_own(1).start()
    plane_start(2)
    z_wait(0)
    plane_start(0)
    plane_wait(2)
    z_start(2, Z_ORDER)
    z_own(2).start()
    plane_wait(0)
    plane_start(3)
    root_exchange(0)
    root_section(0)
    if LOOP:
        plane_wait(3)
        z_start(3, Z_ORDER)
        z_own(3).start()

        @pl.loop(1, CHUNKS)
        def _(c):
            root_z_last(c)
    else:
        root_section(1)
        plane_wait(3)
        z_start(3, NEAR)
        z_start(3, FAR)
        z_own(3).start()
        root_section(2)
        root_section(3)

    for c in range(CHUNKS):
        for k in range(4):
            pair_copy(c, (z + k) % 4, k).wait_send()
        for d in Z_ORDER:
            z_copy(c, d).wait_send()
        plane_all(c).wait_send()
        for k in range(NZ):
            pair2_copy(c, k, k).wait_send()


def per_device(vectors, leaf_factors, root_factors):
    vectors = vectors.reshape(BLOCKS, BLK, CHUNKS * COLS)
    dma = pltpu.SemaphoreType.DMA
    wide_shape = (CHUNKS, BLOCKS, BLK, COLS)
    spread = (CHUNKS, NZ, PLANE, ROWS, COLS)
    halves = (CHUNKS, 2, BLOCKS // 2, BLK, COLS)
    bf = jnp.bfloat16
    vmem = pltpu.VMEM
    out = pl.pallas_call(
        kernel,
        out_shape=jax.ShapeDtypeStruct(vectors.shape, bf),
        in_specs=[pl.BlockSpec(memory_space=pltpu.HBM)] * 3,
        out_specs=pl.BlockSpec(memory_space=pltpu.VMEM),
        scratch_shapes=[
            vmem((LEVELS, BLOCKS, BLK, 2 * BLK), bf),
            vmem((LEVELS, BLOCKS, BLK, 2 * BLK), bf),
            vmem(wide_shape, bf), vmem(halves, bf), vmem(halves, bf),
            vmem(spread, bf), vmem(spread, bf), vmem(spread, bf), vmem(spread, bf),
            vmem(wide_shape[1:], bf), vmem(wide_shape[1:], bf),
            dma((CHUNKS,)), dma((LEVELS,)), dma((LEVELS,)), dma((CHUNKS, 2)),
            dma((CHUNKS, 4)), dma((CHUNKS, 4)), dma((CHUNKS, NZ - 1)), dma((CHUNKS, NZ - 1)),
            dma((CHUNKS,)), dma((CHUNKS,)), dma((CHUNKS, NZ)), dma((CHUNKS, NZ)),
        ],
        compiler_params=pltpu.CompilerParams(
            collective_id=0, has_side_effects=True, vmem_limit_bytes=48 * 1024 * 1024),
        name="butterfly",
    )(in_hbm(vectors), in_hbm(leaf_factors), in_hbm(root_factors))
    return out.reshape(BLOCKS * BLK, CHUNKS * COLS)


def solution(mesh):
    in_specs = (
        P(("wide", "narrow"), None),
        P(None, ("wide", "narrow"), None, None),
        P(None, ("wide", "narrow"), None, None),
    )
    out_specs = P(("wide", "narrow"), None)
    return jax.shard_map(
        per_device, mesh=mesh, in_specs=in_specs, out_specs=out_specs, check_vma=False
    )
```

```python
import jax
import jax.numpy as jnp
from jax import lax
from jax.experimental import pallas as pl
from jax.experimental.pallas import tpu as pltpu
from jax.sharding import PartitionSpec as P

MESH = pl.DeviceIdType.MESH
NZ, NY, NX = 8, 4, 4
PLANE = NY * NX
BLOCKS, BLK, ROWS, COLS, CHUNKS = 32, 64, 16, 128, 4
GROUP = BLOCKS // NZ
LEVELS = 6
PLANE_FIRST = (False, True, True, True)
Z_ORDER = (4, 5, 3, 1, 7, 2, 6)
FAR, NEAR = (4, 5, 3), (1, 7, 2, 6)
BATCHES = ((0,) + NEAR + FAR,)
EARLY = 4
UNROLL = 16
LATE = 2


def in_hbm(array):
    return pltpu.with_memory_space_constraint(array, pltpu.HBM)


RUN = ("L0", "L1", "L2", "L3", "P", "R0", "R1", "R2", "R3")
own_copy = pltpu.make_async_copy


def plane_first(c):
    return PLANE_FIRST[c] if isinstance(c, int) else True


def swap_halves(factor):
    return jnp.concatenate([factor[:, BLK:], factor[:, :BLK]], axis=1)


def product(factor, blocks):
    return jnp.dot(factor, blocks, preferred_element_type=jnp.float32).astype(jnp.bfloat16)


def pair_level(factors, source, target, low, stride):
    high = low + stride
    out = product(
        jnp.concatenate([factors[low], factors[high]], axis=0),
        jnp.concatenate([source[low], source[high]], axis=0),
    )
    target[low] = out[:BLK]
    target[high] = out[BLK:]


def first_of_pair(index, stride):
    return (index // stride) * (2 * stride) + index % stride


def kernel(
    vectors, leaf_hbm, root_hbm, out,
    leaf, root, ping, pong, other, leafed, half, moved, moved_other, ping2, pong2,
    sem_vec, sem_leaf, sem_root, sem_own,
    pair_send, pair_recv, z_send, z_recv, plane_send, plane_recv, pair2_send, pair2_recv,
):
    wide = lax.axis_index("wide")
    core = lax.axis_index("narrow")
    z, y, x = wide // PLANE, (wide // NX) % NY, wide % NX
    plane = wide % PLANE
    partner = (wide, 1 - core)

    def at_z(offset):
        return (z + offset) % NZ

    def z_device(offset):
        return (at_z(offset) * PLANE + plane, core)

    def plane_at(offset):
        return ((y + offset // NX) % NY) * NX + (x + offset % NX) % NX

    def plane_device(offset):
        return (z * PLANE + plane_at(offset), core)

    def load_vec(c):
        return pltpu.make_async_copy(
            vectors.at[:, :, pl.ds(c * COLS, COLS)], ping.at[c], sem_vec.at[c])

    def load_leaf(l):
        return pltpu.make_async_copy(leaf_hbm.at[l], leaf.at[l], sem_leaf.at[l])

    def load_root(l):
        return pltpu.make_async_copy(root_hbm.at[l], root.at[l], sem_root.at[l])

    load_vec(0).start()
    for l in range(EARLY):
        load_leaf(l).start()

    barrier = pltpu.get_barrier_semaphore()
    pl.semaphore_signal(barrier, inc=1, device_id=partner, device_id_type=MESH)
    for d in range(1, NZ):
        pl.semaphore_signal(barrier, inc=1, device_id=z_device(d), device_id_type=MESH)

    @pl.loop(1, PLANE)
    def _(j):
        pl.semaphore_signal(barrier, inc=1, device_id=plane_device(j), device_id_type=MESH)

    def prepare(factors, stride):
        for q in range(BLOCKS // 2):
            high = first_of_pair(q, stride) + stride
            factors[high] = swap_halves(factors[high])

    def pair_copy(c, i, k):
        return pltpu.make_async_remote_copy(
            pong.at[c, :, pl.ds(i * GROUP, GROUP)], other.at[c, :, pl.ds(i * GROUP, GROUP)],
            pair_send.at[c, k], pair_recv.at[c, k], device_id=partner, device_id_type=MESH)

    def z_copy(c, d):
        source, target = (half, moved) if plane_first(c) else (leafed, half)
        return pltpu.make_async_remote_copy(
            source.at[c, at_z(d)], target.at[c, z], z_send.at[c, d - 1], z_recv.at[c, d - 1],
            device_id=z_device(d), device_id_type=MESH)

    def z_own(c):
        source, target = (half, moved) if plane_first(c) else (leafed, half)
        return own_copy(source.at[c, z], target.at[c, z], sem_own.at[c, 0])

    def plane_copy(c, j):
        source, target = (leafed, half) if plane_first(c) else (half, moved)
        return pltpu.make_async_remote_copy(
            source.at[c, :, plane_at(j)], target.at[c, :, plane], plane_send.at[c], plane_recv.at[c],
            device_id=plane_device(j), device_id_type=MESH)

    def plane_all(c):
        source, target = (leafed, half) if plane_first(c) else (half, moved)
        return pltpu.make_async_remote_copy(
            source.at[c, :, pl.ds(0, PLANE - 1)], target.at[c, :, pl.ds(0, PLANE - 1)],
            plane_send.at[c], plane_recv.at[c], device_id=partner, device_id_type=MESH)

    def plane_own(c):
        source, target = (leafed, half) if plane_first(c) else (half, moved)
        return own_copy(source.at[c, :, plane], target.at[c, :, plane], sem_own.at[c, 1])

    def plane_start(c):
        @pl.loop(1, PLANE)
        def _(j):
            plane_copy(c, j).start()
        plane_own(c).start()

    def plane_wait(c):
        plane_own(c).wait()
        plane_all(c).wait_recv()

    def z_start(c, offsets):
        for d in offsets:
            z_copy(c, d).start()

    def pair2_copy(c, zs, k):
        return pltpu.make_async_remote_copy(
            moved.at[c, zs], moved_other.at[c, zs], pair2_send.at[c, k], pair2_recv.at[c, k],
            device_id=partner, device_id_type=MESH)

    def whole_level(factors, source, target, stride):
        if UNROLL == 16:
            for q in range(BLOCKS // 2):
                pair_level(factors, source, target, first_of_pair(q, stride), stride)
            return

        @pl.loop(0, BLOCKS // 2 // UNROLL)
        def _(i):
            for q in range(UNROLL):
                pair_level(factors, source, target, first_of_pair(i * UNROLL + q, stride), stride)

    def leaf_levels(c):
        load_vec(c).wait()
        for l in range(4):
            if c == 0:
                load_leaf(l).wait()
                if l == 0:
                    for m in range(EARLY, LEVELS):
                        load_leaf(m).start()
                prepare(leaf.at[l], 1 << l)
            a = ping.at[c] if l % 2 == 0 else pong.at[c].reshape(BLOCKS, BLK, COLS)
            b = pong.at[c].reshape(BLOCKS, BLK, COLS) if l % 2 == 0 else ping.at[c]
            whole_level(leaf.at[l], a, b, 1 << l)
        if c == 0:
            load_leaf(4).wait()
            prepare(leaf.at[4], 16)
            load_leaf(5).wait()
            for m in range(1, CHUNKS):
                load_vec(m).start()
            pl.semaphore_wait(barrier, 1 + (NZ - 1) + (PLANE - 1))
        for k in range(4):
            i = (z + k) % 4
            for q in range(GROUP):
                pair_level(leaf.at[4], ping.at[c], pong.at[c].reshape(BLOCKS, BLK, COLS), i * GROUP + q, 16)
            pair_copy(c, i, k).start()

    def leaf_last(c):
        mine = pong.at[c].reshape(BLOCKS, BLK, COLS)
        theirs = other.at[c].reshape(BLOCKS, BLK, COLS)
        target = leafed.at[c].reshape(BLOCKS, BLK, COLS)
        for k, offsets in enumerate(((4,), (5, 1), (6, 2), (7, 3, 0))):
            pair_copy(c, (z + k) % 4, k).wait_recv()
            for d in offsets:
                for q in range(GROUP):
                    b = at_z(d) * GROUP + q
                    target[b] = product(leaf[5, b], jnp.concatenate([mine[b], theirs[b]], axis=0))
                if d != 0 and not PLANE_FIRST[c]:
                    z_copy(c, d).start()
        if not PLANE_FIRST[c]:
            z_own(c).start()

    def root_groups(c, groups):
        mine = moved.at[c].reshape(BLOCKS, BLK, COLS)
        theirs = moved_other.at[c].reshape(BLOCKS, BLK, COLS)
        for zs in groups:
            for q in range(GROUP):
                b = zs * GROUP + q
                ping2[b] = product(root[0, b], jnp.concatenate([mine[b], theirs[b]], axis=0))
        for zs in groups:
            for q in (0, 2):
                pair_level(root.at[1], ping2, pong2, zs * GROUP + q, 1)
        for zs in groups:
            for q in (0, 1):
                pair_level(root.at[2], pong2, ping2, zs * GROUP + q, 2)

    def root_rest(c):
        whole_level(root.at[3], ping2, pong2, 4)
        whole_level(root.at[4], pong2, ping2, 8)
        whole_level(root.at[5], ping2, out.at[:, :, pl.ds(pl.multiple_of(c * COLS, COLS) if not isinstance(c, int) else c * COLS, COLS)], 16)

    def root_exchange(c):
        for k in range(NZ):
            pair2_copy(c, k, k).start()

    def root_plane_last(c):
        for batch in (range(4), range(4, 8)):
            for k in batch:
                pair2_copy(c, k, k).wait_recv()
            root_groups(c, batch)
        root_rest(c)

    def root_z_last(c):
        z_own(c).wait()
        pair2_copy(c, z, 0).start()
        for d in NEAR + FAR:
            z_copy(c, d).wait_recv()
            pair2_copy(c, (z - d) % NZ, d).start()
        for d in (0,) + NEAR + FAR:
            pair2_copy(c, (z - d) % NZ, d).wait_recv()
        root_groups(c, range(NZ))
        root_rest(c)

    def z_wait(c):
        z_own(c).wait()
        for d in Z_ORDER:
            z_copy(c, d).wait_recv()

    def leaf_section(c):
        if f"L{c}" in RUN:
            leaf_levels(c)
            leaf_last(c)
        else:
            load_vec(c).wait()
            if c == 0:
                for l in range(LEVELS):
                    load_leaf(l).wait()

    def root_section(c):
        if f"R{c}" in RUN:
            (root_z_last if plane_first(c) else root_plane_last)(c)

    leaf_section(0)
    for l in range(LEVELS):
        load_root(l).start()
    leaf_section(1)
    plane_start(1)
    leaf_section(2)
    leaf_section(3)
    for l in range(LEVELS):
        load_root(l).wait()
        if l and "P" in RUN:
            prepare(root.at[l], 1 << (l - 1))
    plane_wait(1)
    z_start(1, Z_ORDER)
    z_own(1).start()
    plane_start(2)
    z_wait(0)
    plane_start(0)
    plane_wait(2)
    z_start(2, Z_ORDER)
    z_own(2).start()
    plane_wait(0)
    plane_start(3)
    root_exchange(0)
    root_section(0)
    plane_wait(3)
    z_own(3).start()
    if not LATE:
        z_start(3, Z_ORDER)
    else:
        @pl.when(core == 0)
        def _():
            z_start(3, Z_ORDER)

    @pl.loop(1, CHUNKS)
    def _(c):
        root_z_last(c)
        if LATE:
            @pl.when((core == 1) & (c == LATE))
            def _():
                z_start(3, Z_ORDER)

    for c in range(CHUNKS):
        for k in range(4):
            pair_copy(c, (z + k) % 4, k).wait_send()
        for d in Z_ORDER:
            z_copy(c, d).wait_send()
        plane_all(c).wait_send()
        for k in range(NZ):
            pair2_copy(c, k, k).wait_send()


def per_device(vectors, leaf_factors, root_factors):
    vectors = vectors.reshape(BLOCKS, BLK, CHUNKS * COLS)
    dma = pltpu.SemaphoreType.DMA
    wide_shape = (CHUNKS, BLOCKS, BLK, COLS)
    spread = (CHUNKS, NZ, PLANE, ROWS, COLS)
    halves = (CHUNKS, 2, BLOCKS // 2, BLK, COLS)
    bf = jnp.bfloat16
    vmem = pltpu.VMEM
    out = pl.pallas_call(
        kernel,
        out_shape=jax.ShapeDtypeStruct(vectors.shape, bf),
        in_specs=[pl.BlockSpec(memory_space=pltpu.HBM)] * 3,
        out_specs=pl.BlockSpec(memory_space=pltpu.VMEM),
        scratch_shapes=[
            vmem((LEVELS, BLOCKS, BLK, 2 * BLK), bf),
            vmem((LEVELS, BLOCKS, BLK, 2 * BLK), bf),
            vmem(wide_shape, bf), vmem(halves, bf), vmem(halves, bf),
            vmem(spread, bf), vmem(spread, bf), vmem(spread, bf), vmem(spread, bf),
            vmem(wide_shape[1:], bf), vmem(wide_shape[1:], bf),
            dma((CHUNKS,)), dma((LEVELS,)), dma((LEVELS,)), dma((CHUNKS, 2)),
            dma((CHUNKS, 4)), dma((CHUNKS, 4)), dma((CHUNKS, NZ - 1)), dma((CHUNKS, NZ - 1)),
            dma((CHUNKS,)), dma((CHUNKS,)), dma((CHUNKS, NZ)), dma((CHUNKS, NZ)),
        ],
        compiler_params=pltpu.CompilerParams(
            collective_id=0, has_side_effects=True, vmem_limit_bytes=48 * 1024 * 1024),
        name="butterfly",
    )(in_hbm(vectors), in_hbm(leaf_factors), in_hbm(root_factors))
    return out.reshape(BLOCKS * BLK, CHUNKS * COLS)


def solution(mesh):
    in_specs = (
        P(("wide", "narrow"), None),
        P(None, ("wide", "narrow"), None, None),
        P(None, ("wide", "narrow"), None, None),
    )
    out_specs = P(("wide", "narrow"), None)
    return jax.shard_map(
        per_device, mesh=mesh, in_specs=in_specs, out_specs=out_specs, check_vma=False
    )
```

```python
import jax
import jax.numpy as jnp
from jax import lax
from jax.experimental import pallas as pl
from jax.experimental.pallas import tpu as pltpu
from jax.sharding import PartitionSpec as P

MESH = pl.DeviceIdType.MESH
NZ, NY, NX = 8, 4, 4
PLANE = NY * NX
BLOCKS, BLK, ROWS, COLS, CHUNKS = 32, 64, 16, 128, 4
GROUP = BLOCKS // NZ
LEVELS = 6
PLANE_FIRST = (False, True, True, True)
Z_ORDER = (4, 3, 5, 2, 6, 1, 7)
FAR, NEAR = (4, 5, 3), (1, 7, 2, 6)
BATCHES = ((0,) + NEAR + FAR,)
EARLY = 4
UNROLL = 16
LATE = 2


def in_hbm(array):
    return pltpu.with_memory_space_constraint(array, pltpu.HBM)


RUN = ("L0", "L1", "L2", "L3", "P", "R0", "R1", "R2", "R3")
own_copy = pltpu.make_async_copy


def plane_first(c):
    return PLANE_FIRST[c] if isinstance(c, int) else True


def swap_halves(factor):
    return jnp.concatenate([factor[:, BLK:], factor[:, :BLK]], axis=1)


def product(factor, blocks):
    return jnp.dot(factor, blocks, preferred_element_type=jnp.float32).astype(jnp.bfloat16)


def pair_level(factors, source, target, low, stride):
    high = low + stride
    out = product(
        jnp.concatenate([factors[low], factors[high]], axis=0),
        jnp.concatenate([source[low], source[high]], axis=0),
    )
    target[low] = out[:BLK]
    target[high] = out[BLK:]


def first_of_pair(index, stride):
    return (index // stride) * (2 * stride) + index % stride


def kernel(
    vectors, leaf_hbm, root_hbm, out,
    leaf, root, ping, pong, other, leafed, half, moved, moved_other, ping2, pong2,
    sem_vec, sem_leaf, sem_root, sem_own,
    pair_send, pair_recv, z_send, z_recv, plane_send, plane_recv, pair2_send, pair2_recv,
):
    wide = lax.axis_index("wide")
    core = lax.axis_index("narrow")
    z, y, x = wide // PLANE, (wide // NX) % NY, wide % NX
    plane = wide % PLANE
    partner = (wide, 1 - core)

    def at_z(offset):
        return (z + offset) % NZ

    def z_device(offset):
        return (at_z(offset) * PLANE + plane, core)

    def plane_at(offset):
        return ((y + offset // NX) % NY) * NX + (x + offset % NX) % NX

    def plane_device(offset):
        return (z * PLANE + plane_at(offset), core)

    def load_vec(c):
        return pltpu.make_async_copy(
            vectors.at[:, :, pl.ds(c * COLS, COLS)], ping.at[c], sem_vec.at[c])

    def load_leaf(l):
        return pltpu.make_async_copy(leaf_hbm.at[l], leaf.at[l], sem_leaf.at[l])

    def load_root(l):
        return pltpu.make_async_copy(root_hbm.at[l], root.at[l], sem_root.at[l])

    load_vec(0).start()
    for l in range(EARLY):
        load_leaf(l).start()

    barrier = pltpu.get_barrier_semaphore()
    pl.semaphore_signal(barrier, inc=1, device_id=partner, device_id_type=MESH)
    for d in range(1, NZ):
        pl.semaphore_signal(barrier, inc=1, device_id=z_device(d), device_id_type=MESH)

    @pl.loop(1, PLANE)
    def _(j):
        pl.semaphore_signal(barrier, inc=1, device_id=plane_device(j), device_id_type=MESH)

    def prepare(factors, stride):
        for q in range(BLOCKS // 2):
            high = first_of_pair(q, stride) + stride
            factors[high] = swap_halves(factors[high])

    def pair_copy(c, i, k):
        return pltpu.make_async_remote_copy(
            pong.at[c, :, pl.ds(i * GROUP, GROUP)], other.at[c, :, pl.ds(i * GROUP, GROUP)],
            pair_send.at[c, k], pair_recv.at[c, k], device_id=partner, device_id_type=MESH)

    def z_copy(c, d):
        source, target = (half, moved) if plane_first(c) else (leafed, half)
        return pltpu.make_async_remote_copy(
            source.at[c, at_z(d)], target.at[c, z], z_send.at[c, d - 1], z_recv.at[c, d - 1],
            device_id=z_device(d), device_id_type=MESH)

    def z_own(c):
        source, target = (half, moved) if plane_first(c) else (leafed, half)
        return own_copy(source.at[c, z], target.at[c, z], sem_own.at[c, 0])

    def plane_copy(c, j):
        source, target = (leafed, half) if plane_first(c) else (half, moved)
        return pltpu.make_async_remote_copy(
            source.at[c, :, plane_at(j)], target.at[c, :, plane], plane_send.at[c], plane_recv.at[c],
            device_id=plane_device(j), device_id_type=MESH)

    def plane_all(c):
        source, target = (leafed, half) if plane_first(c) else (half, moved)
        return pltpu.make_async_remote_copy(
            source.at[c, :, pl.ds(0, PLANE - 1)], target.at[c, :, pl.ds(0, PLANE - 1)],
            plane_send.at[c], plane_recv.at[c], device_id=partner, device_id_type=MESH)

    def plane_own(c):
        source, target = (leafed, half) if plane_first(c) else (half, moved)
        return own_copy(source.at[c, :, plane], target.at[c, :, plane], sem_own.at[c, 1])

    def plane_start(c):
        @pl.loop(1, PLANE)
        def _(j):
            plane_copy(c, j).start()
        plane_own(c).start()

    def plane_wait(c):
        plane_own(c).wait()
        plane_all(c).wait_recv()

    def z_start(c, offsets):
        for d in offsets:
            z_copy(c, d).start()

    def pair2_copy(c, zs, k):
        return pltpu.make_async_remote_copy(
            moved.at[c, zs], moved_other.at[c, zs], pair2_send.at[c, k], pair2_recv.at[c, k],
            device_id=partner, device_id_type=MESH)

    def whole_level(factors, source, target, stride):
        if UNROLL == 16:
            for q in range(BLOCKS // 2):
                pair_level(factors, source, target, first_of_pair(q, stride), stride)
            return

        @pl.loop(0, BLOCKS // 2 // UNROLL)
        def _(i):
            for q in range(UNROLL):
                pair_level(factors, source, target, first_of_pair(i * UNROLL + q, stride), stride)

    def leaf_levels(c):
        load_vec(c).wait()
        for l in range(4):
            if c == 0:
                load_leaf(l).wait()
                if l == 0:
                    for m in range(EARLY, LEVELS):
                        load_leaf(m).start()
                prepare(leaf.at[l], 1 << l)
            a = ping.at[c] if l % 2 == 0 else pong.at[c].reshape(BLOCKS, BLK, COLS)
            b = pong.at[c].reshape(BLOCKS, BLK, COLS) if l % 2 == 0 else ping.at[c]
            whole_level(leaf.at[l], a, b, 1 << l)
        if c == 0:
            load_leaf(4).wait()
            prepare(leaf.at[4], 16)
            load_leaf(5).wait()
            for m in range(1, CHUNKS):
                load_vec(m).start()
        whole_level(leaf.at[4], ping.at[c], pong.at[c].reshape(BLOCKS, BLK, COLS), 16)
        if c == 0:
            pl.semaphore_wait(barrier, 1 + (NZ - 1) + (PLANE - 1))
        for i in range(4):
            pair_copy(c, i, i).start()

    def leaf_last(c):
        mine = pong.at[c].reshape(BLOCKS, BLK, COLS)
        theirs = other.at[c].reshape(BLOCKS, BLK, COLS)
        target = leafed.at[c].reshape(BLOCKS, BLK, COLS)
        for i in range(4):
            pair_copy(c, i, i).wait_recv()
            for to in (i, i + 4):
                for q in range(GROUP):
                    b = to * GROUP + q
                    target[b] = product(leaf[5, b], jnp.concatenate([mine[b], theirs[b]], axis=0))
            if not PLANE_FIRST[c]:
                for to in (i, i + 4):
                    @pl.when(z != to)
                    def _():
                        z_copy(c, (to - z) % NZ).start()
        if not PLANE_FIRST[c]:
            z_own(c).start()

    def root_groups(c, groups):
        mine = moved.at[c].reshape(BLOCKS, BLK, COLS)
        theirs = moved_other.at[c].reshape(BLOCKS, BLK, COLS)
        for zs in groups:
            for q in range(GROUP):
                b = zs * GROUP + q
                ping2[b] = product(root[0, b], jnp.concatenate([mine[b], theirs[b]], axis=0))
        for zs in groups:
            for q in (0, 2):
                pair_level(root.at[1], ping2, pong2, zs * GROUP + q, 1)
        for zs in groups:
            for q in (0, 1):
                pair_level(root.at[2], pong2, ping2, zs * GROUP + q, 2)

    def root_rest(c):
        whole_level(root.at[3], ping2, pong2, 4)
        whole_level(root.at[4], pong2, ping2, 8)
        whole_level(root.at[5], ping2, out.at[:, :, pl.ds(pl.multiple_of(c * COLS, COLS) if not isinstance(c, int) else c * COLS, COLS)], 16)

    def root_exchange(c):
        for k in range(NZ):
            pair2_copy(c, k, k).start()

    def root_plane_last(c):
        for batch in (range(4), range(4, 8)):
            for k in batch:
                pair2_copy(c, k, k).wait_recv()
            root_groups(c, batch)
        root_rest(c)

    def root_z_last(c):
        z_own(c).wait()
        pair2_copy(c, z, 0).start()
        for d in NEAR + FAR:
            z_copy(c, d).wait_recv()
            pair2_copy(c, (z - d) % NZ, d).start()
        for d in (0,) + NEAR + FAR:
            pair2_copy(c, (z - d) % NZ, d).wait_recv()
        root_groups(c, range(NZ))
        root_rest(c)

    def z_wait(c):
        z_own(c).wait()
        for d in Z_ORDER:
            z_copy(c, d).wait_recv()

    def leaf_section(c):
        if f"L{c}" in RUN:
            leaf_levels(c)
            leaf_last(c)
        else:
            load_vec(c).wait()
            if c == 0:
                for l in range(LEVELS):
                    load_leaf(l).wait()

    def root_section(c):
        if f"R{c}" in RUN:
            (root_z_last if plane_first(c) else root_plane_last)(c)

    leaf_section(0)
    for l in range(LEVELS):
        load_root(l).start()
    leaf_section(1)
    plane_start(1)
    leaf_section(2)
    leaf_section(3)
    for l in range(LEVELS):
        load_root(l).wait()
        if l and "P" in RUN:
            prepare(root.at[l], 1 << (l - 1))
    plane_wait(1)
    z_start(1, Z_ORDER)
    z_own(1).start()
    plane_start(2)
    z_wait(0)
    plane_start(0)
    plane_wait(2)
    z_start(2, Z_ORDER)
    z_own(2).start()
    plane_wait(0)
    plane_start(3)
    root_exchange(0)
    root_section(0)
    plane_wait(3)
    z_own(3).start()
    if not LATE:
        z_start(3, Z_ORDER)
    else:
        @pl.when(core == 0)
        def _():
            z_start(3, Z_ORDER)

    @pl.loop(1, CHUNKS)
    def _(c):
        root_z_last(c)
        if LATE:
            @pl.when((core == 1) & (c == LATE))
            def _():
                z_start(3, Z_ORDER)

    for c in range(CHUNKS):
        for k in range(4):
            pair_copy(c, k, k).wait_send()
        for d in Z_ORDER:
            z_copy(c, d).wait_send()
        plane_all(c).wait_send()
        for k in range(NZ):
            pair2_copy(c, k, k).wait_send()


def per_device(vectors, leaf_factors, root_factors):
    vectors = vectors.reshape(BLOCKS, BLK, CHUNKS * COLS)
    dma = pltpu.SemaphoreType.DMA
    wide_shape = (CHUNKS, BLOCKS, BLK, COLS)
    spread = (CHUNKS, NZ, PLANE, ROWS, COLS)
    halves = (CHUNKS, 2, BLOCKS // 2, BLK, COLS)
    bf = jnp.bfloat16
    vmem = pltpu.VMEM
    out = pl.pallas_call(
        kernel,
        out_shape=jax.ShapeDtypeStruct(vectors.shape, bf),
        in_specs=[pl.BlockSpec(memory_space=pltpu.HBM)] * 3,
        out_specs=pl.BlockSpec(memory_space=pltpu.VMEM),
        scratch_shapes=[
            vmem((LEVELS, BLOCKS, BLK, 2 * BLK), bf),
            vmem((LEVELS, BLOCKS, BLK, 2 * BLK), bf),
            vmem(wide_shape, bf), vmem(halves, bf), vmem(halves, bf),
            vmem(spread, bf), vmem(spread, bf), vmem(spread, bf), vmem(spread, bf),
            vmem(wide_shape[1:], bf), vmem(wide_shape[1:], bf),
            dma((CHUNKS,)), dma((LEVELS,)), dma((LEVELS,)), dma((CHUNKS, 2)),
            dma((CHUNKS, 4)), dma((CHUNKS, 4)), dma((CHUNKS, NZ - 1)), dma((CHUNKS, NZ - 1)),
            dma((CHUNKS,)), dma((CHUNKS,)), dma((CHUNKS, NZ)), dma((CHUNKS, NZ)),
        ],
        compiler_params=pltpu.CompilerParams(
            collective_id=0, has_side_effects=True, vmem_limit_bytes=48 * 1024 * 1024),
        name="butterfly",
    )(in_hbm(vectors), in_hbm(leaf_factors), in_hbm(root_factors))
    return out.reshape(BLOCKS * BLK, CHUNKS * COLS)


def solution(mesh):
    in_specs = (
        P(("wide", "narrow"), None),
        P(None, ("wide", "narrow"), None, None),
        P(None, ("wide", "narrow"), None, None),
    )
    out_specs = P(("wide", "narrow"), None)
    return jax.shard_map(
        per_device, mesh=mesh, in_specs=in_specs, out_specs=out_specs, check_vma=False
    )
```

```python
import jax
import jax.numpy as jnp
from jax import lax
from jax.experimental import pallas as pl
from jax.experimental.pallas import tpu as pltpu
from jax.sharding import PartitionSpec as P

MESH = pl.DeviceIdType.MESH
NZ, NY, NX = 8, 4, 4
PLANE = NY * NX
BLOCKS, BLK, ROWS, COLS, CHUNKS = 32, 64, 16, 128, 4
GROUP = BLOCKS // NZ
LEVELS = 6
PLANE_FIRST = (False, True, True, True)
Z_ORDER = (4, 3, 5, 2, 6, 1, 7)
FAR, NEAR = (4, 5, 3), (1, 7, 2, 6)
BATCHES = ((0,) + NEAR + FAR,)
EARLY = 4
UNROLL = 16
LATE = 2


def in_hbm(array):
    return pltpu.with_memory_space_constraint(array, pltpu.HBM)


RUN = ("L0", "L1", "L2", "L3", "P", "R0", "R1", "R2", "R3")
own_copy = pltpu.make_async_copy


def plane_first(c):
    return PLANE_FIRST[c] if isinstance(c, int) else True


def swap_halves(factor):
    return jnp.concatenate([factor[:, BLK:], factor[:, :BLK]], axis=1)


def product(factor, blocks):
    return jnp.dot(factor, blocks, preferred_element_type=jnp.float32).astype(jnp.bfloat16)


def pair_level(factors, source, target, low, stride):
    high = low + stride
    out = product(
        jnp.concatenate([factors[low], factors[high]], axis=0),
        jnp.concatenate([source[low], source[high]], axis=0),
    )
    target[low] = out[:BLK]
    target[high] = out[BLK:]


def first_of_pair(index, stride):
    return (index // stride) * (2 * stride) + index % stride


def kernel(
    vectors, leaf_hbm, root_hbm, out,
    leaf, root, ping, pong, other, leafed, half, moved, moved_other, ping2, pong2,
    sem_vec, sem_leaf, sem_root, sem_own,
    pair_send, pair_recv, z_send, z_recv, plane_send, plane_recv, pair2_send, pair2_recv,
):
    wide = lax.axis_index("wide")
    core = lax.axis_index("narrow")
    z, y, x = wide // PLANE, (wide // NX) % NY, wide % NX
    plane = wide % PLANE
    partner = (wide, 1 - core)

    def at_z(offset):
        return (z + offset) % NZ

    def z_device(offset):
        return (at_z(offset) * PLANE + plane, core)

    def plane_at(offset):
        return ((y + offset // NX) % NY) * NX + (x + offset % NX) % NX

    def plane_device(offset):
        return (z * PLANE + plane_at(offset), core)

    def load_vec(c):
        return pltpu.make_async_copy(
            vectors.at[:, :, pl.ds(c * COLS, COLS)], ping.at[c], sem_vec.at[c])

    def load_leaf(l):
        return pltpu.make_async_copy(leaf_hbm.at[l], leaf.at[l], sem_leaf.at[l])

    def load_root(l):
        return pltpu.make_async_copy(root_hbm.at[l], root.at[l], sem_root.at[l])

    load_vec(0).start()
    for l in range(EARLY):
        load_leaf(l).start()

    barrier = pltpu.get_barrier_semaphore()
    pl.semaphore_signal(barrier, inc=1, device_id=partner, device_id_type=MESH)
    for d in range(1, NZ):
        pl.semaphore_signal(barrier, inc=1, device_id=z_device(d), device_id_type=MESH)

    @pl.loop(1, PLANE)
    def _(j):
        pl.semaphore_signal(barrier, inc=1, device_id=plane_device(j), device_id_type=MESH)

    def prepare(factors, stride):
        for q in range(BLOCKS // 2):
            high = first_of_pair(q, stride) + stride
            factors[high] = swap_halves(factors[high])

    def pair_copy(c, i, k):
        return pltpu.make_async_remote_copy(
            pong.at[c, :, pl.ds(i * GROUP, GROUP)], other.at[c, :, pl.ds(i * GROUP, GROUP)],
            pair_send.at[c, k], pair_recv.at[c, k], device_id=partner, device_id_type=MESH)

    def z_copy(c, d):
        source, target = (half, moved) if plane_first(c) else (leafed, half)
        return pltpu.make_async_remote_copy(
            source.at[c, at_z(d)], target.at[c, z], z_send.at[c, d - 1], z_recv.at[c, d - 1],
            device_id=z_device(d), device_id_type=MESH)

    def z_own(c):
        source, target = (half, moved) if plane_first(c) else (leafed, half)
        return own_copy(source.at[c, z], target.at[c, z], sem_own.at[c, 0])

    def plane_copy(c, j):
        source, target = (leafed, half) if plane_first(c) else (half, moved)
        return pltpu.make_async_remote_copy(
            source.at[c, :, plane_at(j)], target.at[c, :, plane], plane_send.at[c], plane_recv.at[c],
            device_id=plane_device(j), device_id_type=MESH)

    def plane_all(c):
        source, target = (leafed, half) if plane_first(c) else (half, moved)
        return pltpu.make_async_remote_copy(
            source.at[c, :, pl.ds(0, PLANE - 1)], target.at[c, :, pl.ds(0, PLANE - 1)],
            plane_send.at[c], plane_recv.at[c], device_id=partner, device_id_type=MESH)

    def plane_own(c):
        source, target = (leafed, half) if plane_first(c) else (half, moved)
        return own_copy(source.at[c, :, plane], target.at[c, :, plane], sem_own.at[c, 1])

    def plane_start(c):
        @pl.loop(1, PLANE)
        def _(j):
            plane_copy(c, j).start()
        plane_own(c).start()

    def plane_wait(c):
        plane_own(c).wait()
        plane_all(c).wait_recv()

    def z_start(c, offsets):
        for d in offsets:
            z_copy(c, d).start()

    def pair2_copy(c, zs, k):
        return pltpu.make_async_remote_copy(
            moved.at[c, zs], moved_other.at[c, zs], pair2_send.at[c, k], pair2_recv.at[c, k],
            device_id=partner, device_id_type=MESH)

    def whole_level(factors, source, target, stride):
        if UNROLL == 16:
            for q in range(BLOCKS // 2):
                pair_level(factors, source, target, first_of_pair(q, stride), stride)
            return

        @pl.loop(0, BLOCKS // 2 // UNROLL)
        def _(i):
            for q in range(UNROLL):
                pair_level(factors, source, target, first_of_pair(i * UNROLL + q, stride), stride)

    def leaf_levels(c):
        load_vec(c).wait()
        for l in range(4):
            if c == 0:
                load_leaf(l).wait()
                if l == 0:
                    for m in range(EARLY, LEVELS):
                        load_leaf(m).start()
                prepare(leaf.at[l], 1 << l)
            a = ping.at[c] if l % 2 == 0 else pong.at[c].reshape(BLOCKS, BLK, COLS)
            b = pong.at[c].reshape(BLOCKS, BLK, COLS) if l % 2 == 0 else ping.at[c]
            whole_level(leaf.at[l], a, b, 1 << l)
        if c == 0:
            load_leaf(4).wait()
            prepare(leaf.at[4], 16)
            load_leaf(5).wait()
            for m in range(1, CHUNKS):
                load_vec(m).start()
        whole_level(leaf.at[4], ping.at[c], pong.at[c].reshape(BLOCKS, BLK, COLS), 16)
        if c == 0:
            pl.semaphore_wait(barrier, 1 + (NZ - 1) + (PLANE - 1))
        for i in range(4):
            pair_copy(c, i, i).start()

    def leaf_last(c):
        mine = pong.at[c].reshape(BLOCKS, BLK, COLS)
        theirs = other.at[c].reshape(BLOCKS, BLK, COLS)
        target = leafed.at[c].reshape(BLOCKS, BLK, COLS)
        for i in range(4):
            pair_copy(c, i, i).wait_recv()
            for to in (i, i + 4):
                for q in range(GROUP):
                    b = to * GROUP + q
                    target[b] = product(leaf[5, b], jnp.concatenate([mine[b], theirs[b]], axis=0))
            if not PLANE_FIRST[c]:
                for to in (i, i + 4):
                    @pl.when(z != to)
                    def _():
                        z_copy(c, (to - z) % NZ).start()
        if not PLANE_FIRST[c]:
            z_own(c).start()

    def root_groups(c, groups):
        mine = moved.at[c].reshape(BLOCKS, BLK, COLS)
        theirs = moved_other.at[c].reshape(BLOCKS, BLK, COLS)
        for zs in groups:
            for q in range(GROUP):
                b = zs * GROUP + q
                ping2[b] = product(root[0, b], jnp.concatenate([mine[b], theirs[b]], axis=0))
        for zs in groups:
            for q in (0, 2):
                pair_level(root.at[1], ping2, pong2, zs * GROUP + q, 1)
        for zs in groups:
            for q in (0, 1):
                pair_level(root.at[2], pong2, ping2, zs * GROUP + q, 2)

    def root_rest(c):
        whole_level(root.at[3], ping2, pong2, 4)
        whole_level(root.at[4], pong2, ping2, 8)
        whole_level(root.at[5], ping2, out.at[:, :, pl.ds(pl.multiple_of(c * COLS, COLS) if not isinstance(c, int) else c * COLS, COLS)], 16)

    def root_exchange(c):
        for k in range(NZ):
            pair2_copy(c, k, k).start()

    def root_plane_last(c):
        for batch in (range(4), range(4, 8)):
            for k in batch:
                pair2_copy(c, k, k).wait_recv()
            root_groups(c, batch)
        root_rest(c)

    def root_z_last(c):
        z_own(c).wait()
        pair2_copy(c, z, 0).start()
        for d in NEAR + FAR:
            z_copy(c, d).wait_recv()
            pair2_copy(c, (z - d) % NZ, d).start()
        for d in (0,) + NEAR + FAR:
            pair2_copy(c, (z - d) % NZ, d).wait_recv()
        root_groups(c, range(NZ))
        root_rest(c)

    def z_wait(c):
        z_own(c).wait()
        for d in Z_ORDER:
            z_copy(c, d).wait_recv()

    def leaf_section(c):
        if f"L{c}" in RUN:
            leaf_levels(c)
            leaf_last(c)
        else:
            load_vec(c).wait()
            if c == 0:
                for l in range(LEVELS):
                    load_leaf(l).wait()

    def root_section(c):
        if f"R{c}" in RUN:
            (root_z_last if plane_first(c) else root_plane_last)(c)

    leaf_section(0)
    for l in range(LEVELS):
        load_root(l).start()
    leaf_section(1)
    plane_start(1)
    leaf_section(2)
    leaf_section(3)
    for l in range(LEVELS):
        load_root(l).wait()
        if l and "P" in RUN:
            prepare(root.at[l], 1 << (l - 1))
    plane_wait(1)
    z_start(1, Z_ORDER)
    z_own(1).start()
    plane_start(2)
    z_wait(0)
    plane_start(0)
    plane_wait(2)
    z_start(2, Z_ORDER)
    z_own(2).start()
    plane_wait(0)
    plane_start(3)
    root_exchange(0)
    root_section(0)
    plane_wait(3)
    z_own(3).start()
    if not LATE:
        z_start(3, Z_ORDER)
    else:
        @pl.when(core == 0)
        def _():
            z_start(3, Z_ORDER)

    def sent(c):
        for d in Z_ORDER:
            z_copy(c, d).wait_send()
        for k in range(NZ):
            pair2_copy(c, k, k).wait_send()

    for c in range(CHUNKS):
        for k in range(4):
            pair_copy(c, k, k).wait_send()
        plane_all(c).wait_send()
    sent(0)

    @pl.loop(1, CHUNKS)
    def _(c):
        root_z_last(c)
        if LATE:
            @pl.when((core == 1) & (c == LATE))
            def _():
                z_start(3, Z_ORDER)

        sent(c)


def per_device(vectors, leaf_factors, root_factors):
    vectors = vectors.reshape(BLOCKS, BLK, CHUNKS * COLS)
    dma = pltpu.SemaphoreType.DMA
    wide_shape = (CHUNKS, BLOCKS, BLK, COLS)
    spread = (CHUNKS, NZ, PLANE, ROWS, COLS)
    halves = (CHUNKS, 2, BLOCKS // 2, BLK, COLS)
    bf = jnp.bfloat16
    vmem = pltpu.VMEM
    out = pl.pallas_call(
        kernel,
        out_shape=jax.ShapeDtypeStruct(vectors.shape, bf),
        in_specs=[pl.BlockSpec(memory_space=pltpu.HBM)] * 3,
        out_specs=pl.BlockSpec(memory_space=pltpu.VMEM),
        scratch_shapes=[
            vmem((LEVELS, BLOCKS, BLK, 2 * BLK), bf),
            vmem((LEVELS, BLOCKS, BLK, 2 * BLK), bf),
            vmem(wide_shape, bf), vmem(halves, bf), vmem(halves, bf),
            vmem(spread, bf), vmem(spread, bf), vmem(spread, bf), vmem(spread, bf),
            vmem(wide_shape[1:], bf), vmem(wide_shape[1:], bf),
            dma((CHUNKS,)), dma((LEVELS,)), dma((LEVELS,)), dma((CHUNKS, 2)),
            dma((CHUNKS, 4)), dma((CHUNKS, 4)), dma((CHUNKS, NZ - 1)), dma((CHUNKS, NZ - 1)),
            dma((CHUNKS,)), dma((CHUNKS,)), dma((CHUNKS, NZ)), dma((CHUNKS, NZ)),
        ],
        compiler_params=pltpu.CompilerParams(
            collective_id=0, has_side_effects=True, vmem_limit_bytes=48 * 1024 * 1024),
        name="butterfly",
    )(in_hbm(vectors), in_hbm(leaf_factors), in_hbm(root_factors))
    return out.reshape(BLOCKS * BLK, CHUNKS * COLS)


def solution(mesh):
    in_specs = (
        P(("wide", "narrow"), None),
        P(None, ("wide", "narrow"), None, None),
        P(None, ("wide", "narrow"), None, None),
    )
    out_specs = P(("wide", "narrow"), None)
    return jax.shard_map(
        per_device, mesh=mesh, in_specs=in_specs, out_specs=out_specs, check_vma=False
    )
```

```python
import jax
import jax.numpy as jnp
from jax import lax
from jax.experimental import pallas as pl
from jax.experimental.pallas import tpu as pltpu
from jax.sharding import PartitionSpec as P

MESH = pl.DeviceIdType.MESH
NZ, NY, NX = 8, 4, 4
PLANE = NY * NX
BLOCKS, BLK, ROWS, COLS, CHUNKS = 32, 64, 16, 128, 4
GROUP = BLOCKS // NZ
LEVELS = 6
PLANE_FIRST = (False, True, True, True)
Z_ORDER = (4, 3, 5, 2, 6, 1, 7)
FAR, NEAR = (4, 5, 3), (1, 7, 2, 6)
BATCHES = ((0,) + NEAR + FAR,)
EARLY = 4
UNROLL = 16
LATE = 2


def in_hbm(array):
    return pltpu.with_memory_space_constraint(array, pltpu.HBM)


RUN = ("L0", "L1", "L2", "L3", "P", "R0", "R1", "R2", "R3")
own_copy = pltpu.make_async_copy


def plane_first(c):
    return PLANE_FIRST[c] if isinstance(c, int) else True


def swap_halves(factor):
    return jnp.concatenate([factor[:, BLK:], factor[:, :BLK]], axis=1)


def product(factor, blocks):
    return jnp.dot(factor, blocks, preferred_element_type=jnp.float32).astype(jnp.bfloat16)


def pair_level(factors, source, target, low, stride):
    high = low + stride
    out = product(
        jnp.concatenate([factors[low], factors[high]], axis=0),
        jnp.concatenate([source[low], source[high]], axis=0),
    )
    target[low] = out[:BLK]
    target[high] = out[BLK:]


def first_of_pair(index, stride):
    return (index // stride) * (2 * stride) + index % stride


def kernel(
    vectors, leaf_hbm, root_hbm, out,
    leaf, root, ping, pong, other, leafed, half, moved, moved_other, ping2, pong2,
    sem_vec, sem_leaf, sem_root, sem_own,
    pair_send, pair_recv, z_send, z_recv, plane_send, plane_recv, pair2_send, pair2_recv,
):
    wide = lax.axis_index("wide")
    core = lax.axis_index("narrow")
    z, y, x = wide // PLANE, (wide // NX) % NY, wide % NX
    plane = wide % PLANE
    partner = (wide, 1 - core)

    def at_z(offset):
        return (z + offset) % NZ

    def z_device(offset):
        return (at_z(offset) * PLANE + plane, core)

    def plane_at(offset):
        return ((y + offset // NX) % NY) * NX + (x + offset % NX) % NX

    def plane_device(offset):
        return (z * PLANE + plane_at(offset), core)

    def load_vec(c):
        return pltpu.make_async_copy(
            vectors.at[:, :, pl.ds(c * COLS, COLS)], ping.at[c], sem_vec.at[c])

    def load_leaf(l):
        return pltpu.make_async_copy(leaf_hbm.at[l], leaf.at[l], sem_leaf.at[l])

    def load_root(l):
        return pltpu.make_async_copy(root_hbm.at[l], root.at[l], sem_root.at[l])

    load_vec(0).start()
    for l in range(EARLY):
        load_leaf(l).start()

    barrier = pltpu.get_barrier_semaphore()
    pl.semaphore_signal(barrier, inc=1, device_id=partner, device_id_type=MESH)
    for d in range(1, NZ):
        pl.semaphore_signal(barrier, inc=1, device_id=z_device(d), device_id_type=MESH)

    @pl.loop(1, PLANE)
    def _(j):
        pl.semaphore_signal(barrier, inc=1, device_id=plane_device(j), device_id_type=MESH)

    def prepare(factors, stride):
        for q in range(BLOCKS // 2):
            high = first_of_pair(q, stride) + stride
            factors[high] = swap_halves(factors[high])

    def pair_copy(c, i, k):
        return pltpu.make_async_remote_copy(
            pong.at[c, :, pl.ds(i * GROUP, GROUP)], other.at[c, :, pl.ds(i * GROUP, GROUP)],
            pair_send.at[c, k], pair_recv.at[c, k], device_id=partner, device_id_type=MESH)

    def z_copy(c, d):
        source, target = (half, moved) if plane_first(c) else (leafed, half)
        return pltpu.make_async_remote_copy(
            source.at[c, at_z(d)], target.at[c, z], z_send.at[c, d - 1], z_recv.at[c, d - 1],
            device_id=z_device(d), device_id_type=MESH)

    def z_own(c):
        source, target = (half, moved) if plane_first(c) else (leafed, half)
        return own_copy(source.at[c, z], target.at[c, z], sem_own.at[c, 0])

    def plane_copy(c, j):
        source, target = (leafed, half) if plane_first(c) else (half, moved)
        return pltpu.make_async_remote_copy(
            source.at[c, :, plane_at(j)], target.at[c, :, plane], plane_send.at[c], plane_recv.at[c],
            device_id=plane_device(j), device_id_type=MESH)

    def plane_all(c):
        source, target = (leafed, half) if plane_first(c) else (half, moved)
        return pltpu.make_async_remote_copy(
            source.at[c, :, pl.ds(0, PLANE - 1)], target.at[c, :, pl.ds(0, PLANE - 1)],
            plane_send.at[c], plane_recv.at[c], device_id=partner, device_id_type=MESH)

    def plane_own(c):
        source, target = (leafed, half) if plane_first(c) else (half, moved)
        return own_copy(source.at[c, :, plane], target.at[c, :, plane], sem_own.at[c, 1])

    def plane_start(c):
        @pl.loop(1, PLANE)
        def _(j):
            plane_copy(c, j).start()
        plane_own(c).start()

    def plane_wait(c):
        plane_own(c).wait()
        plane_all(c).wait_recv()

    def z_start(c, offsets):
        for d in offsets:
            z_copy(c, d).start()

    def pair2_copy(c, zs, k):
        return pltpu.make_async_remote_copy(
            moved.at[c, zs], moved_other.at[c, zs], pair2_send.at[c, k], pair2_recv.at[c, k],
            device_id=partner, device_id_type=MESH)

    def whole_level(factors, source, target, stride):
        if UNROLL == 16:
            for q in range(BLOCKS // 2):
                pair_level(factors, source, target, first_of_pair(q, stride), stride)
            return

        @pl.loop(0, BLOCKS // 2 // UNROLL)
        def _(i):
            for q in range(UNROLL):
                pair_level(factors, source, target, first_of_pair(i * UNROLL + q, stride), stride)

    def leaf_levels(c):
        load_vec(c).wait()
        for l in range(4):
            if c == 0:
                load_leaf(l).wait()
                if l == 0:
                    for m in range(EARLY, LEVELS):
                        load_leaf(m).start()
                prepare(leaf.at[l], 1 << l)
            a = ping.at[c] if l % 2 == 0 else pong.at[c].reshape(BLOCKS, BLK, COLS)
            b = pong.at[c].reshape(BLOCKS, BLK, COLS) if l % 2 == 0 else ping.at[c]
            whole_level(leaf.at[l], a, b, 1 << l)
        if c == 0:
            load_leaf(4).wait()
            prepare(leaf.at[4], 16)
            load_leaf(5).wait()
            for m in range(1, CHUNKS):
                load_vec(m).start()
        whole_level(leaf.at[4], ping.at[c], pong.at[c].reshape(BLOCKS, BLK, COLS), 16)
        if c == 0:
            pl.semaphore_wait(barrier, 1 + (NZ - 1) + (PLANE - 1))
        for k in (0, 1, 3, 2):
            i = (z + k) % 4
            pair_copy(c, i, i).start()

    def leaf_last(c):
        mine = pong.at[c].reshape(BLOCKS, BLK, COLS)
        theirs = other.at[c].reshape(BLOCKS, BLK, COLS)
        target = leafed.at[c].reshape(BLOCKS, BLK, COLS)
        for k in (0, 1, 3, 2):
            i = (z + k) % 4
            pair_copy(c, i, i).wait_recv()
            for d in (k, k + 4):
                for q in range(GROUP):
                    b = at_z(d) * GROUP + q
                    target[b] = product(leaf[5, b], jnp.concatenate([mine[b], theirs[b]], axis=0))
            if not PLANE_FIRST[c]:
                z_start(c, {0: (4,), 1: (5,), 3: (3,), 2: (2, 6, 1, 7)}[k])
        if not PLANE_FIRST[c]:
            z_own(c).start()

    def root_groups(c, groups):
        mine = moved.at[c].reshape(BLOCKS, BLK, COLS)
        theirs = moved_other.at[c].reshape(BLOCKS, BLK, COLS)
        for zs in groups:
            for q in range(GROUP):
                b = zs * GROUP + q
                ping2[b] = product(root[0, b], jnp.concatenate([mine[b], theirs[b]], axis=0))
        for zs in groups:
            for q in (0, 2):
                pair_level(root.at[1], ping2, pong2, zs * GROUP + q, 1)
        for zs in groups:
            for q in (0, 1):
                pair_level(root.at[2], pong2, ping2, zs * GROUP + q, 2)

    def root_rest(c):
        whole_level(root.at[3], ping2, pong2, 4)
        whole_level(root.at[4], pong2, ping2, 8)
        whole_level(root.at[5], ping2, out.at[:, :, pl.ds(pl.multiple_of(c * COLS, COLS) if not isinstance(c, int) else c * COLS, COLS)], 16)

    def root_exchange(c):
        for k in range(NZ):
            pair2_copy(c, k, k).start()

    def root_plane_last(c):
        for batch in (range(4), range(4, 8)):
            for k in batch:
                pair2_copy(c, k, k).wait_recv()
            root_groups(c, batch)
        root_rest(c)

    def root_z_last(c):
        z_own(c).wait()
        pair2_copy(c, z, 0).start()
        for d in NEAR + FAR:
            z_copy(c, d).wait_recv()
            pair2_copy(c, (z - d) % NZ, d).start()
        for d in (0,) + NEAR + FAR:
            pair2_copy(c, (z - d) % NZ, d).wait_recv()
        root_groups(c, range(NZ))
        root_rest(c)

    def z_wait(c):
        z_own(c).wait()
        for d in Z_ORDER:
            z_copy(c, d).wait_recv()

    def leaf_section(c):
        if f"L{c}" in RUN:
            leaf_levels(c)
            leaf_last(c)
        else:
            load_vec(c).wait()
            if c == 0:
                for l in range(LEVELS):
                    load_leaf(l).wait()

    def root_section(c):
        if f"R{c}" in RUN:
            (root_z_last if plane_first(c) else root_plane_last)(c)

    leaf_section(0)
    for l in range(LEVELS):
        load_root(l).start()
    leaf_section(1)
    plane_start(1)
    leaf_section(2)
    leaf_section(3)
    for l in range(LEVELS):
        load_root(l).wait()
        if l and "P" in RUN:
            prepare(root.at[l], 1 << (l - 1))
    plane_wait(1)
    z_start(1, Z_ORDER)
    z_own(1).start()
    plane_start(2)
    z_wait(0)
    plane_start(0)
    plane_wait(2)
    z_start(2, Z_ORDER)
    z_own(2).start()
    plane_wait(0)
    plane_start(3)
    root_exchange(0)
    root_section(0)
    plane_wait(3)
    z_own(3).start()
    if not LATE:
        z_start(3, Z_ORDER)
    else:
        @pl.when(core == 0)
        def _():
            z_start(3, Z_ORDER)

    def sent(c):
        for d in Z_ORDER:
            z_copy(c, d).wait_send()
        for k in range(NZ):
            pair2_copy(c, k, k).wait_send()

    for c in range(CHUNKS):
        for k in range(4):
            pair_copy(c, k, k).wait_send()
        plane_all(c).wait_send()
    sent(0)

    @pl.loop(1, CHUNKS)
    def _(c):
        root_z_last(c)
        if LATE:
            @pl.when((core == 1) & (c == LATE))
            def _():
                z_start(3, Z_ORDER)

        sent(c)


def per_device(vectors, leaf_factors, root_factors):
    vectors = vectors.reshape(BLOCKS, BLK, CHUNKS * COLS)
    dma = pltpu.SemaphoreType.DMA
    wide_shape = (CHUNKS, BLOCKS, BLK, COLS)
    spread = (CHUNKS, NZ, PLANE, ROWS, COLS)
    halves = (CHUNKS, 2, BLOCKS // 2, BLK, COLS)
    bf = jnp.bfloat16
    vmem = pltpu.VMEM
    out = pl.pallas_call(
        kernel,
        out_shape=jax.ShapeDtypeStruct(vectors.shape, bf),
        in_specs=[pl.BlockSpec(memory_space=pltpu.HBM)] * 3,
        out_specs=pl.BlockSpec(memory_space=pltpu.VMEM),
        scratch_shapes=[
            vmem((LEVELS, BLOCKS, BLK, 2 * BLK), bf),
            vmem((LEVELS, BLOCKS, BLK, 2 * BLK), bf),
            vmem(wide_shape, bf), vmem(halves, bf), vmem(halves, bf),
            vmem(spread, bf), vmem(spread, bf), vmem(spread, bf), vmem(spread, bf),
            vmem(wide_shape[1:], bf), vmem(wide_shape[1:], bf),
            dma((CHUNKS,)), dma((LEVELS,)), dma((LEVELS,)), dma((CHUNKS, 2)),
            dma((CHUNKS, 4)), dma((CHUNKS, 4)), dma((CHUNKS, NZ - 1)), dma((CHUNKS, NZ - 1)),
            dma((CHUNKS,)), dma((CHUNKS,)), dma((CHUNKS, NZ)), dma((CHUNKS, NZ)),
        ],
        compiler_params=pltpu.CompilerParams(
            collective_id=0, has_side_effects=True, vmem_limit_bytes=48 * 1024 * 1024),
        name="butterfly",
    )(in_hbm(vectors), in_hbm(leaf_factors), in_hbm(root_factors))
    return out.reshape(BLOCKS * BLK, CHUNKS * COLS)


def solution(mesh):
    in_specs = (
        P(("wide", "narrow"), None),
        P(None, ("wide", "narrow"), None, None),
        P(None, ("wide", "narrow"), None, None),
    )
    out_specs = P(("wide", "narrow"), None)
    return jax.shard_map(
        per_device, mesh=mesh, in_specs=in_specs, out_specs=out_specs, check_vma=False
    )
```
